32 devices in a mesh: group: 4 (over z), shard: 8 (over y, x, core).
Axes of the slice: x: 2, y: 2, z: 4, core: 2. Of those that a mesh axis runs over, the one named last changes fastest.
Arguments:
- queries: bfloat16 [2, 3, 4096, 512], P(None, None, ('group', 'shard')), may hold values from -6 to 6
- key_tokens: bfloat16 [2, 3, 4096, 512], P(None, None, ('group', 'shard')), may hold values from -6 to 6
- value_tokens: bfloat16 [2, 3, 4096, 512], P(None, None, ('group', 'shard')), may hold values from -6 to 6
- token_rate: float32 [2, 3, 4096], P(None, None, ('group', 'shard')), may hold values from 0.1 to 1
- state_in: float32 [4, 3, 512, 3, 512], P('group', None, 'shard'), may hold values from -0.25 to 0.25
- init_state: float32 [3, 512, 3, 512], P(None, 'shard'), may hold values from -0.25 to 0.25
- norm_gain: float32 [3, 512], replicated, may hold values from 0.25 to 2.5
Outputs:
- head_output: bfloat16 [2, 3, 4096, 512], P(None, None, ('group', 'shard'))
- state_out: float32 [4, 3, 512, 3, 512], P('group', None, 'shard')
The draws below stay inside these ranges and needn't reach their ends.
All inputs are finite; a program needn't handle non-finite values.
Results may differ from the reference program's by a relative error of at most 0.011.
Values may be sent and summed in bfloat16 or wider, within the bound.
No kernel may reach another device: no remote copies, remote signals or barrier semaphores. Data moves between devices by JAX's collectives and lax.ppermute only.
A program may use at most 128 MiB of HBM per device.

```python
import math
import jax
import jax.numpy as jnp
from jax import lax

D = 512
FH = 512
HEADS = 3
TOK_DEV = 128
SECTIONS = 4
TOKENS = 4096
N_GROUP = 4
N_SHARD = 8


def raised(drawn, rng, source, target, shards_of, factor):
    def block_of(axis_at):
        return (jnp.arange(drawn.shape[axis_at]) // (drawn.shape[axis_at] // shards_of)).reshape((-1,) + (1,) * (drawn.ndim - 1 - axis_at))

    near = jax.random.permutation(rng, shards_of)[block_of(target)]
    second = (block_of(target) + shards_of // 2) % shards_of
    return jnp.where((block_of(source) == near) | (block_of(source) == second), factor * drawn, drawn)


def steps_of(own_key, dims, shards, least, high):
    loudness, own = 1.0, jax.random.fold_in(own_key, 6)
    for axis_at, parts in shards:
        steps = jnp.exp(jax.random.uniform(jax.random.fold_in(own, axis_at), (parts,), jnp.float32, least / len(shards), high / len(shards)))
        loudness = loudness * jnp.repeat(steps, dims[axis_at] // parts).reshape([-1 if axis == axis_at else 1 for axis in range(len(dims))])
    return loudness


def normal_values(key, shape, spread, bound, split=(), kind=jnp.bfloat16):
    array = jax.random.normal(key, shape, jnp.float32) * spread
    if len(split) > 0:
        array = steps_of(key, shape, split, -0.22, 0.18) * array
    return jnp.clip(array, min=-bound, max=bound).astype(kind)


def noise_with(stream_key, shape, spread, bound, split, heavy, held_as=jnp.bfloat16):
    result = spread * jax.random.normal(stream_key, shape, jnp.float32)
    if split:
        result = result * steps_of(stream_key, shape, split, -0.22, 0.18)
    return jnp.clip(raised(result, jax.random.fold_in(stream_key, 3), *heavy), -bound, bound).astype(held_as)


def setup_inputs(seed: int = 0) -> dict:
    key_list = jax.random.split(jax.random.key(seed), 8)
    return {
        "queries": normal_values(key_list[0], (2, HEADS, TOKENS, D), 1.0, 6.0, ((2, 32),)),
        "key_tokens": noise_with(key_list[1], (2, HEADS, TOKENS, D), 1.0, 6.0, ((2, 32),), (2, 3, 32, 2.75)),
        "value_tokens": noise_with(key_list[2], (2, HEADS, TOKENS, D), 1.0, 6.0, ((2, 32),), (2, 3, 32, 2.75)),
        "token_rate": jnp.clip(jnp.exp(math.log(1.0) - 2.3025851 * jax.random.uniform(key_list[3], (2, HEADS, TOKENS), jnp.float32) ** steps_of(key_list[3], (2, HEADS, TOKENS), ((2, 32),), -0.2, 0.2)), 0.1, 1.0),
        "state_in": normal_values(key_list[4], (SECTIONS, HEADS, D, 3, FH), D ** -0.5, 0.25, ((0, 4), (2, 8)), jnp.float32),
        "init_state": normal_values(key_list[5], (HEADS, D, 3, FH), D ** -0.5, 0.25, ((1, 8),), jnp.float32),
        "norm_gain": jnp.clip(jnp.exp(jax.random.uniform(key_list[6], (HEADS, D), jnp.float32, math.log(0.25), math.log(2.5))), 0.25, 2.5),
    }


epsilon = 1e-06

def forward(rows, packed):
    pre_gate = jnp.dot(rows, packed[:, 0], preferred_element_type=jnp.float32)
    pre_up = jnp.dot(rows, packed[:, 1], preferred_element_type=jnp.float32)
    sigmoid_gate = jax.nn.sigmoid(pre_gate)
    hidden = (pre_gate * sigmoid_gate * pre_up).astype(jnp.bfloat16)
    produced = lax.dot_general(hidden, packed[:, 2], (((1,), (1,)), ((), ())), preferred_element_type=jnp.float32)
    return (pre_gate, pre_up, sigmoid_gate, hidden, produced)

def section_head(weights, query_rows, key_rows, value_rows, rate_row, gain_row):
    packed = weights.astype(jnp.bfloat16)
    applied = forward(query_rows, packed)[4]
    normed = applied * lax.rsqrt(lax.optimization_barrier(jnp.mean(applied * applied, axis=-1, keepdims=True)) + epsilon) * gain_row
    pre_gate, pre_up, sigmoid_gate, hidden, guess = forward(key_rows, packed)
    error = (rate_row[:, None] * (guess - value_rows.astype(jnp.float32))).astype(jnp.bfloat16)
    back_hidden = jnp.dot(error, packed[:, 2], preferred_element_type=jnp.float32)
    grad_gate = (back_hidden * pre_up * sigmoid_gate * (1.0 + pre_gate * (1.0 - sigmoid_gate))).astype(jnp.bfloat16)
    grad_up = (back_hidden * pre_gate * sigmoid_gate).astype(jnp.bfloat16)
    contract = (((0,), (0,)), ((), ()))
    gate_part = lax.dot_general(key_rows, grad_gate, contract, preferred_element_type=jnp.float32)
    up_part = lax.dot_general(key_rows, grad_up, contract, preferred_element_type=jnp.float32)
    down_part = lax.dot_general(error, hidden, contract, preferred_element_type=jnp.float32)
    summed = jnp.stack([gate_part, up_part, down_part], axis=1)
    updated = weights - summed / float(TOK_DEV * N_SHARD)
    return (normed.astype(jnp.bfloat16), updated)

def reference(queries, key_tokens, value_tokens, token_rate, state_in, init_state, norm_gain):
    span = TOK_DEV * N_SHARD

    def slot_pass(slot_index, weights_all):

        def per_section(section_index):
            begin = (section_index * span).astype(jnp.int32)

            def per_head(head_index):
                query_rows = lax.dynamic_slice_in_dim(queries[slot_index][head_index], begin, span, 0)
                key_rows = lax.dynamic_slice_in_dim(key_tokens[slot_index][head_index], begin, span, 0)
                value_rows = lax.dynamic_slice_in_dim(value_tokens[slot_index][head_index], begin, span, 0)
                rate_row = lax.dynamic_slice_in_dim(token_rate[slot_index][head_index], begin, span, 0)
                return section_head(weights_all[section_index][head_index], query_rows, key_rows, value_rows, rate_row, norm_gain[head_index])
            return lax.map(per_head, jnp.arange(HEADS, dtype=jnp.int32))
        outputs, updated = lax.map(per_section, jnp.arange(N_GROUP, dtype=jnp.int32))
        outputs = jnp.transpose(outputs, (1, 0, 2, 3)).reshape(HEADS, TOKENS, D)
        return (outputs, updated)
    first_out, middle = slot_pass(0, state_in)
    arrived = jnp.concatenate([init_state[None], middle[:-1]], axis=0)
    second_out, final = slot_pass(1, arrived)
    return (jnp.stack([first_out, second_out], axis=0), final)
```

```python
import functools

import jax
import jax.numpy as jnp
import numpy as np
from jax import lax
from jax.experimental import pallas as pl
from jax.experimental.pallas import tpu as pltpu
from jax.sharding import Mesh
from jax.sharding import PartitionSpec as P

EPSILON = 1e-06
RATE_ROWS = 16
BF16 = jnp.bfloat16
F32 = jnp.float32
TRANS_A = (((0,), (0,)), ((), ()))
TRANS_B = (((1,), (1,)), ((), ()))
VMEM = pl.BlockSpec(memory_space=pltpu.VMEM)
SMEM = pl.BlockSpec(memory_space=pltpu.SMEM)
PARAMS = pltpu.CompilerParams(vmem_limit_bytes=48 * 1024 * 1024)


def mm(left, right):
    return jnp.dot(left, right, preferred_element_type=F32)


def column(rows, tokens):
    total = rows[:1, :tokens].astype(F32) + rows[:1, tokens : 2 * tokens].astype(F32)
    spread = jnp.broadcast_to(total, (tokens, tokens))
    across = lax.broadcasted_iota(jnp.int32, (tokens, tokens), 0)
    down = lax.broadcasted_iota(jnp.int32, (tokens, tokens), 1)
    return jnp.sum(jnp.where(across == down, spread, 0.0), axis=1, keepdims=True)


def hidden_of(rows, weights):
    width = weights.shape[1] // 2
    both = mm(rows, weights)
    gate, up = both[:, :width], both[:, width:]
    sig = jax.nn.sigmoid(gate)
    return gate, up, sig, (gate * sig * up).astype(BF16)


def apply_norm(rows, gate_up, down, gain):
    hidden = hidden_of(rows, gate_up)[3]
    out = lax.dot_general(hidden, down, TRANS_B, preferred_element_type=F32)
    scale = lax.rsqrt(jnp.mean(out * out, axis=-1, keepdims=True) + EPSILON)
    return (out * scale * gain).astype(BF16)


def gradients(keys, values, rates, gate_up, down):
    gate, up, sig, hidden = hidden_of(keys, gate_up)
    guess = lax.dot_general(hidden, down, TRANS_B, preferred_element_type=F32)
    error = (rates * (guess - values.astype(F32))).astype(BF16)
    back = mm(error, down)
    d_gate = (back * up * sig * (1.0 + gate * (1.0 - sig))).astype(BF16)
    d_up = (back * gate * sig).astype(BF16)
    return error, hidden, jnp.concatenate([d_gate, d_up], axis=1)


def pieces_of(ref, start, count):
    value = ref[:, start : start + count, :]
    return value.reshape(value.shape[0] * count, value.shape[2])


def rates_of(ref, start, tokens):
    return jnp.concatenate(
        [column(ref[piece, start : start + RATE_ROWS, :], tokens) for piece in range(ref.shape[0])], 0
    )


def lay_rows(refs, start, rows, core, cores, width, gate_up, down):
    chips = refs[0].shape[0]
    for which, ref in enumerate(refs):
        owner = core if which == 0 else cores - 1 - core
        for chip in range(chips):
            at = pl.ds(pl.multiple_of((chip * cores + owner) * rows, rows), rows)
            gate_up[at, :width] = ref[chip, start : start + rows, :]
            gate_up[at, width:] = ref[chip, start + rows : start + 2 * rows, :]
            down[at, :] = ref[chip, start + 2 * rows : start + 3 * rows, :]


def first_kernel(cores, groups, tokens, rows, span, place, *refs):
    halves = refs[:cores]
    sent, gate_up, down, sum_gate_up, sum_down, init_gate_up, init_down = refs[cores:]
    width = down.shape[1]
    depth = down.shape[0]
    part = depth // cores
    group, core = place[0], place[2]
    mine = pl.ds(pl.multiple_of(core * part, part), part)
    lay_rows(halves, 2 * tokens, rows, core, cores, width, gate_up, down)

    @pl.when(group == groups - 1)
    def _():
        lay_rows(halves, 0, rows, core, cores, width, init_gate_up, init_down)
        sent[0] = init_gate_up[mine, :width]
        sent[1] = init_gate_up[mine, width:]
        sent[2] = init_down[mine, :]

    @pl.when(group < groups - 1)
    def _():
        for which, ref in enumerate(halves):
            keys = pieces_of(ref, 0, tokens)
            values = pieces_of(ref, tokens, tokens)
            rates = rates_of(ref, 2 * tokens + 3 * rows, tokens)
            error, hidden, d_both = gradients(keys, values, rates, gate_up[...], down[...])
            q_both = lax.dot_general(keys, d_both, TRANS_A, preferred_element_type=F32)
            q_down = lax.dot_general(error, hidden, TRANS_A, preferred_element_type=F32)
            if which == 0:
                sum_gate_up[...] = q_both
                sum_down[...] = q_down
            else:
                sum_gate_up[...] += q_both
                sum_down[...] += q_down
        new_both = (gate_up[mine, :].astype(F32) - sum_gate_up[mine, :] / span).astype(BF16)
        sent[0] = new_both[:, :width]
        sent[1] = new_both[:, width:]
        sent[2] = (down[mine, :].astype(F32) - sum_down[mine, :] / span).astype(BF16)


def query_kernel(tokens, start, place, queries, gate_up, down, gain, out):
    row = gain[pl.ds(jnp.minimum(place[1], gain.shape[0] - 1), 1), :]
    rows = pieces_of(queries, start, tokens)
    out[...] = apply_norm(rows, gate_up[...], down[...], row).reshape(out.shape)


def second_kernel(cores, tokens, rows, span, place, *refs):
    halves = refs[:cores]
    states = refs[cores : 2 * cores]
    queries, gain, applied, updated, gate_up, down, sum_gate_up, sum_down = refs[2 * cores :]
    width = down.shape[1]
    part = states[0].shape[1]
    core = place[2]
    for which, ref in enumerate(states):
        owner = core if which == 0 else cores - 1 - core
        at = pl.ds(pl.multiple_of(owner * part, part), part)
        gate_up[at, :width] = ref[0]
        gate_up[at, width:] = ref[1]
        down[at, :] = ref[2]
    row = gain[pl.ds(jnp.minimum(place[1], gain.shape[0] - 1), 1), :]
    asked = pieces_of(queries, tokens, tokens)
    applied[...] = apply_norm(asked, gate_up[...], down[...], row).reshape(applied.shape)
    for which, ref in enumerate(halves):
        keys = pieces_of(ref, 0, tokens)
        values = pieces_of(ref, tokens, tokens)
        rates = rates_of(ref, 2 * tokens, tokens)
        error, hidden, d_both = gradients(keys, values, rates, gate_up[...], down[...])
        q_both = lax.dot_general(keys, d_both, TRANS_A, preferred_element_type=F32)
        q_down = lax.dot_general(error, hidden, TRANS_A, preferred_element_type=F32)
        if which == 0:
            sum_gate_up[...] = q_both
            sum_down[...] = q_down
        else:
            sum_gate_up[...] += q_both
            sum_down[...] += q_down
    for chip in range(updated.shape[0]):
        at = pl.ds(pl.multiple_of((chip * cores + core) * rows, rows), rows)
        new_both = gate_up[at, :].astype(F32) - sum_gate_up[at, :] / span
        updated[chip, :rows, :] = new_both[:, :width].astype(BF16)
        updated[chip, rows : 2 * rows, :] = new_both[:, width:].astype(BF16)
        new_down = down[at, :].astype(F32) - sum_down[at, :] / span
        updated[chip, 2 * rows :, :] = new_down.astype(BF16)


def rate_rows(rates, width):
    high = lax.reduce_precision(rates, 8, 7)
    low = rates - high
    flat = jnp.concatenate([high, low], axis=-1).astype(BF16)
    flat = jnp.pad(flat, ((0, 0), (0, RATE_ROWS * width - flat.shape[-1])))
    return flat.reshape(flat.shape[0], RATE_ROWS, width)


def on_device(queries, key_tokens, value_tokens, token_rate, state_in, init_state, norm_gain):
    groups, chips, cores = (lax.axis_size(name) for name in ("group", "chip", "core"))
    heads, tokens, depth = queries.shape[1:]
    rows, width = state_in.shape[2], state_in.shape[4]
    span = float(tokens * chips * cores)
    group, chip, core = (lax.axis_index(name) for name in ("group", "chip", "core"))
    place = jnp.stack([group, chip, core]).astype(jnp.int32)

    def by_matrix(state):
        return jnp.transpose(state, (0, 2, 1, 3)).reshape(heads, 3 * rows, width).astype(BF16)

    def to_owners(packed):
        slots = jnp.pad(packed, ((0, chips - heads), (0, 0), (0, 0)))
        return lax.all_to_all(slots, "chip", 0, 0, tiled=True)

    def back(packed):
        return lax.all_to_all(packed, "chip", 0, 0, tiled=True)[:heads]

    def sibling(value):
        return lax.ppermute(value, "core", [(at, cores - 1 - at) for at in range(cores)])

    rates = [rate_rows(token_rate[slot], width) for slot in range(2)]
    learn = jnp.concatenate([key_tokens[0], value_tokens[0]], axis=1)
    start = jnp.pad(by_matrix(init_state), ((0, 0), (0, 2 * tokens - 3 * rows), (0, 0)))
    learn = jnp.where(group == groups - 1, start, learn)
    one = to_owners(jnp.concatenate([learn, by_matrix(state_in[0]), rates[0]], axis=1))
    two = to_owners(jnp.concatenate([key_tokens[1], value_tokens[1], rates[1]], axis=1))
    asked = to_owners(jnp.concatenate([queries[0], queries[1]], axis=1))
    one = (one, sibling(one))

    mats = [
        jax.ShapeDtypeStruct((depth, 2 * width), BF16),
        jax.ShapeDtypeStruct((depth, width), BF16),
    ]
    sums = [pltpu.VMEM((depth, 2 * width), F32), pltpu.VMEM((depth, width), F32)]
    sent, gate_up, down = pl.pallas_call(
        functools.partial(first_kernel, cores, groups, tokens, rows, span),
        out_shape=[jax.ShapeDtypeStruct((3, depth // cores, width), BF16)] + mats,
        in_specs=[SMEM] + [VMEM] * cores,
        out_specs=[VMEM] * 3,
        scratch_shapes=sums + [pltpu.VMEM(mat.shape, BF16) for mat in mats],
        compiler_params=PARAMS,
        name="slot0_keys",
    )(place, *one)
    arrived = lax.ppermute(sent, "group", [(at, (at + 1) % groups) for at in range(groups)])
    two = (two, sibling(two))
    applied0 = pl.pallas_call(
        functools.partial(query_kernel, tokens, 0),
        out_shape=jax.ShapeDtypeStruct((chips, tokens, depth), BF16),
        in_specs=[SMEM] + [VMEM] * 4,
        out_specs=VMEM,
        compiler_params=PARAMS,
        name="slot0_queries",
    )(place, asked, gate_up, down, norm_gain)
    out0 = back(applied0)
    applied1, updated = pl.pallas_call(
        functools.partial(second_kernel, cores, tokens, rows, span),
        out_shape=[
            jax.ShapeDtypeStruct((chips, tokens, depth), BF16),
            jax.ShapeDtypeStruct((chips, 3 * rows, width), BF16),
        ],
        in_specs=[SMEM] + [VMEM] * (2 * cores + 2),
        out_specs=[VMEM] * 2,
        scratch_shapes=[pltpu.VMEM(mat.shape, BF16) for mat in mats] + sums,
        compiler_params=PARAMS,
        name="slot1",
    )(place, *two, arrived, sibling(arrived), asked, norm_gain)
    last = back(jnp.concatenate([applied1, updated], axis=1))
    head_output = jnp.stack([out0, last[:, :tokens]], axis=0)
    state = last[:, tokens:].reshape(heads, 3, rows, width).astype(F32)
    return head_output, jnp.transpose(state, (0, 2, 1, 3))[None]


def solution(mesh):
    groups, shards = mesh.shape["group"], mesh.shape["shard"]
    cores = 2 if shards % 2 == 0 else 1
    devices = np.asarray(mesh.devices).reshape(groups, shards // cores, cores)
    split = Mesh(devices, ("group", "chip", "core"))
    tokens = ("group", "chip", "core")
    shard = ("chip", "core")
    in_specs = (
        P(None, None, tokens, None),
        P(None, None, tokens, None),
        P(None, None, tokens, None),
        P(None, None, tokens),
        P("group", None, shard, None, None),
        P(None, shard, None, None),
        P(),
    )
    out_specs = (P(None, None, tokens, None), P("group", None, shard, None, None))
    return jax.shard_map(
        on_device, mesh=split, in_specs=in_specs, out_specs=out_specs, check_vma=False
    )
```

```python
import functools

import jax
import jax.numpy as jnp
import numpy as np
from jax import lax
from jax.experimental import pallas as pl
from jax.experimental.pallas import tpu as pltpu
from jax.sharding import Mesh
from jax.sharding import PartitionSpec as P

EPSILON = 1e-06
RATE_ROWS = 16
BF16 = jnp.bfloat16
F32 = jnp.float32
TRANS_A = (((0,), (0,)), ((), ()))
TRANS_B = (((1,), (1,)), ((), ()))
VMEM = pl.BlockSpec(memory_space=pltpu.VMEM)
SMEM = pl.BlockSpec(memory_space=pltpu.SMEM)
PARAMS = pltpu.CompilerParams(vmem_limit_bytes=40 * 1024 * 1024)


def target(chip, step, chips):
    if chips & (chips - 1) == 0:
        return chip ^ step
    return (chip + step) % chips


def source(chip, step, chips):
    return target(chip, step if chips & (chips - 1) == 0 else chips - step, chips)


def mm(left, right):
    return jnp.dot(left, right, preferred_element_type=F32)


def mm_ta(left, right):
    return lax.dot_general(left, right, TRANS_A, preferred_element_type=F32)


def mm_tb(left, right):
    return lax.dot_general(left, right, TRANS_B, preferred_element_type=F32)


def rate_block(row, width):
    high = row.astype(BF16)
    low = (row - high.astype(F32)).astype(BF16)
    rest = jnp.zeros((1, width - 2 * row.shape[1]), F32)
    line = jnp.concatenate([high.astype(F32), low.astype(F32), rest], axis=1)
    return jnp.broadcast_to(line, (RATE_ROWS, width)).astype(BF16)


def rate_column(rows, tokens):
    total = rows[:1, :tokens].astype(F32) + rows[:1, tokens : 2 * tokens].astype(F32)
    spread = jnp.broadcast_to(total, (tokens, tokens))
    across = lax.broadcasted_iota(jnp.int32, (tokens, tokens), 0)
    down = lax.broadcasted_iota(jnp.int32, (tokens, tokens), 1)
    return jnp.sum(jnp.where(across == down, spread, 0.0), axis=1, keepdims=True)


def stacked(refs, start, count):
    return jnp.concatenate([ref[start : start + count, :] for ref in refs], axis=0)


def rates_of(refs, start, tokens):
    parts = [rate_column(ref[start : start + RATE_ROWS, :], tokens) for ref in refs]
    return jnp.concatenate(parts, axis=0)


def hidden_of(rows, weights):
    width = weights.shape[1] // 2
    both = mm(rows, weights)
    gate, up = both[:, :width], both[:, width:]
    return both, (gate * jax.nn.sigmoid(gate) * up).astype(BF16)


def apply_norm(rows, gate_up, down, gain):
    out = mm_tb(hidden_of(rows, gate_up)[1], down)
    scale = lax.rsqrt(jnp.mean(out * out, axis=-1, keepdims=True) + EPSILON)
    return (out * scale * gain).astype(BF16)


def backward(both, guess, values, rates, down):
    width = both.shape[1] // 2
    gate, up = both[:, :width], both[:, width:]
    sig = jax.nn.sigmoid(gate)
    error = (rates * (guess - values.astype(F32))).astype(BF16)
    back = mm(error, down)
    d_gate = (back * up * sig * (1.0 + gate * (1.0 - sig))).astype(BF16)
    d_up = (back * gate * sig).astype(BF16)
    return error, jnp.concatenate([d_gate, d_up], axis=1)


def lay_rows(get, rows, place, chips, cores, gate_up, down):
    width = down.shape[1]
    for which in range(cores):
        owner = place[2] if which == 0 else cores - 1 - place[2]
        for step in range(chips):
            chip = source(place[1], step, chips)
            at = pl.ds(pl.multiple_of((chip * cores + owner) * rows, rows), rows)
            gate_up[at, :width] = get(which, step, 0)
            gate_up[at, width:] = get(which, step, rows)
            down[at, :] = get(which, step, 2 * rows)


def pack0_kernel(groups, chips, place, keys, values, rates, state, init, *outs):
    heads, tokens = keys.shape[1:3]
    rows = state.shape[2]
    width = state.shape[3]
    for step in range(chips):
        head = jnp.minimum(target(place[1], step, chips), heads - 1)
        one, two = outs[step], outs[chips + step]
        one[:tokens, :] = keys[0, head]
        for mat in range(3):
            at = tokens + mat * rows
            one[at : at + rows, :] = state[head, mat].astype(BF16)
        two[:tokens, :] = values[0, head]
        two[tokens:, :] = rate_block(rates[0, pl.ds(head, 1), :], width)

        @pl.when(place[0] == groups - 1)
        def _():
            for mat in range(3):
                ref, at = (one, mat * rows) if (mat + 1) * rows <= tokens else (two, 0)
                ref[at : at + rows, :] = init[head, mat].astype(BF16)


def pack1_kernel(chips, place, keys, values, rates, queries, *outs):
    heads, tokens, width = keys.shape[1:]
    for step in range(chips):
        head = jnp.minimum(target(place[1], step, chips), heads - 1)
        learn, ask = outs[step], outs[chips + step]
        learn[:tokens, :] = keys[0, head]
        learn[tokens : 2 * tokens, :] = values[0, head]
        learn[2 * tokens :, :] = rate_block(rates[1, pl.ds(head, 1), :], width)
        ask[:tokens, :] = queries[0, head]
        ask[tokens:, :] = queries[1, head]


def forward_kernel(chips, cores, tokens, rows, place, *refs):
    halves = [refs[which * chips : (which + 1) * chips] for which in range(cores)]
    gate_up, down, both, hidden, guess = refs[cores * chips :]

    def get(which, step, at):
        return halves[which][step][tokens + at : tokens + at + rows, :]

    lay_rows(get, rows, place, chips, cores, gate_up, down)
    count = chips * tokens
    for which in range(cores):
        at = slice(which * count, (which + 1) * count)
        pair, hid = hidden_of(stacked(halves[which], 0, tokens), gate_up[...])
        both[at, :] = pair
        hidden[at, :] = hid
        guess[at, :] = mm_tb(hid, down[...])


def gradient_kernel(groups, chips, cores, tokens, rows, span, place, *refs):
    pieces = chips * cores
    halves = [refs[which * chips : (which + 1) * chips] for which in range(cores)]
    seconds = [refs[pieces + which * chips : pieces + (which + 1) * chips] for which in range(cores)]
    gate_up, down, both, hidden, guess = refs[2 * pieces : 2 * pieces + 5]
    sent, init_gate_up, init_down = refs[2 * pieces + 5 :]
    depth, width = down.shape
    part = depth // cores
    group, core = place[0], place[2]
    mine = pl.ds(pl.multiple_of(core * part, part), part)
    count = chips * tokens

    @pl.when(group == groups - 1)
    def _():
        def get(which, step, at):
            if at + rows <= tokens:
                return halves[which][step][at : at + rows, :]
            return seconds[which][step][:rows, :]

        lay_rows(get, rows, place, chips, cores, init_gate_up, init_down)
        sent[0] = init_gate_up[mine, :width]
        sent[1] = init_gate_up[mine, width:]
        sent[2] = init_down[mine, :]

    @pl.when(group < groups - 1)
    def _():
        new_both = gate_up[mine, :].astype(F32)
        new_down = down[mine, :].astype(F32)
        for which in range(cores):
            at = slice(which * count, (which + 1) * count)
            values = stacked(seconds[which], 0, tokens)
            rates = rates_of(seconds[which], tokens, tokens)
            error, d_both = backward(both[at, :], guess[at, :], values, rates, down[...])
            keys = jnp.concatenate([ref[:tokens, mine] for ref in halves[which]], axis=0)
            picked = error[:, :part]
            for other in range(1, cores):
                picked = jnp.where(core == other, error[:, other * part : (other + 1) * part], picked)
            new_both -= mm_ta(keys, d_both) / span
            new_down -= mm_ta(picked, hidden[at, :]) / span
        sent[0] = new_both[:, :width].astype(BF16)
        sent[1] = new_both[:, width:].astype(BF16)
        sent[2] = new_down.astype(BF16)


def query_kernel(chips, tokens, place, *refs):
    gate_up, down, gain = refs[chips : chips + 3]
    outs = refs[chips + 3 :]
    row = gain[pl.ds(jnp.minimum(place[1], gain.shape[0] - 1), 1), :]
    out = apply_norm(stacked(refs[:chips], 0, tokens), gate_up[...], down[...], row)
    for step in range(chips):
        outs[step][...] = out[step * tokens : (step + 1) * tokens, :]


def second_kernel(chips, cores, tokens, rows, span, place, *refs):
    pieces = chips * cores
    halves = [refs[which * chips : (which + 1) * chips] for which in range(cores)]
    asked = refs[pieces : pieces + chips]
    states = refs[pieces + chips : pieces + chips + cores]
    gain = refs[pieces + chips + cores]
    outs = refs[pieces + chips + cores + 1 : pieces + 3 * chips + cores + 1]
    gate_up, down, sum_both, sum_down = refs[pieces + 3 * chips + cores + 1 :]
    width = down.shape[1]
    part = states[0].shape[1]
    core = place[2]
    for which, ref in enumerate(states):
        owner = core if which == 0 else cores - 1 - core
        at = pl.ds(pl.multiple_of(owner * part, part), part)
        gate_up[at, :width] = ref[0]
        gate_up[at, width:] = ref[1]
        down[at, :] = ref[2]
    row = gain[pl.ds(jnp.minimum(place[1], gain.shape[0] - 1), 1), :]
    applied = apply_norm(stacked(asked, tokens, tokens), gate_up[...], down[...], row)
    for step in range(chips):
        outs[step][...] = applied[step * tokens : (step + 1) * tokens, :]
    for which in range(cores):
        keys = stacked(halves[which], 0, tokens)
        values = stacked(halves[which], tokens, tokens)
        rates = rates_of(halves[which], 2 * tokens, tokens)
        both, hidden = hidden_of(keys, gate_up[...])
        guess = mm_tb(hidden, down[...])
        error, d_both = backward(both, guess, values, rates, down[...])
        q_both, q_down = mm_ta(keys, d_both), mm_ta(error, hidden)
        if which == 0:
            sum_both[...] = q_both
            sum_down[...] = q_down
        else:
            sum_both[...] += q_both
            sum_down[...] += q_down
    for step in range(chips):
        chip = source(place[1], step, chips)
        at = pl.ds(pl.multiple_of((chip * cores + core) * rows, rows), rows)
        out = outs[chips + step]
        new_both = gate_up[at, :].astype(F32) - sum_both[at, :] / span
        out[:rows, :] = new_both[:, :width].astype(BF16)
        out[rows : 2 * rows, :] = new_both[:, width:].astype(BF16)
        out[2 * rows :, :] = (down[at, :].astype(F32) - sum_down[at, :] / span).astype(BF16)


def unpack_kernel(chips, place, *refs):
    zeros, ones, states = refs[:chips], refs[chips : 2 * chips], refs[2 * chips : 3 * chips]
    head_output, state_out = refs[3 * chips :]
    heads, rows = state_out.shape[0], state_out.shape[2]
    for step in range(chips):
        head = target(place[1], step, chips)

        @pl.when(head < heads)
        def _():
            head_output[0, head] = zeros[step][...]
            head_output[1, head] = ones[step][...]
            for mat in range(3):
                state_out[head, mat] = states[step][mat * rows : (mat + 1) * rows, :].astype(F32)


def on_device(queries, key_tokens, value_tokens, token_rate, state_in, init_state, norm_gain):
    groups, chips, cores = (lax.axis_size(name) for name in ("group", "chip", "core"))
    heads, tokens, depth = queries.shape[1:]
    rows, width = state_in.shape[2], state_in.shape[4]
    span = float(tokens * chips * cores)
    group, chip, core = (lax.axis_index(name) for name in ("group", "chip", "core"))
    place = jnp.stack([group, chip, core]).astype(jnp.int32)

    def call(kernel, name, ins, shapes, *operands, scratch=()):
        return pl.pallas_call(
            kernel,
            grid=(1,),
            out_shape=[jax.ShapeDtypeStruct(shape, kind) for shape, kind in shapes],
            in_specs=[SMEM] + ins,
            out_specs=[VMEM] * len(shapes),
            scratch_shapes=list(scratch),
            compiler_params=PARAMS,
            name=name,
        )(place, *operands)

    def slot(number):
        return pl.BlockSpec((1, heads, tokens, depth), lambda at: (number, 0, 0, 0))

    def inward(pieces):
        got = [pieces[0]]
        for step in range(1, chips):
            pairs = [(source(owner, step, chips), owner) for owner in range(heads)]
            got.append(lax.ppermute(pieces[step], "chip", pairs))
        return got

    def outward(pieces):
        got = [pieces[0]]
        for step in range(1, chips):
            pairs = [(owner, source(owner, step, chips)) for owner in range(heads)]
            got.append(lax.ppermute(pieces[step], "chip", pairs))
        return got

    def sibling(value):
        return lax.ppermute(value, "core", [(at, cores - 1 - at) for at in range(cores)])

    state = jnp.transpose(state_in[0], (0, 2, 1, 3))
    init = jnp.transpose(init_state, (0, 2, 1, 3))
    packed = call(
        functools.partial(pack0_kernel, groups, chips),
        "pack_slot0",
        [slot(0), slot(0), VMEM, VMEM, VMEM],
        [((tokens + 3 * rows, depth), BF16)] * chips + [((tokens + RATE_ROWS, depth), BF16)] * chips,
        key_tokens,
        value_tokens,
        token_rate,
        state,
        init,
    )
    first = inward(packed[:chips])
    second = inward(packed[chips:])
    packed = call(
        functools.partial(pack1_kernel, chips),
        "pack_slot1",
        [slot(1), slot(1), VMEM, VMEM],
        [((2 * tokens + RATE_ROWS, depth), BF16)] * chips + [((2 * tokens, depth), BF16)] * chips,
        key_tokens,
        value_tokens,
        token_rate,
        queries,
    )
    learn = inward(packed[:chips])
    asked = inward(packed[chips:])
    first += [sibling(piece) for piece in first]
    second += [sibling(piece) for piece in second]
    learn += [sibling(piece) for piece in learn]

    block = tokens * chips * cores
    kept = call(
        functools.partial(forward_kernel, chips, cores, tokens, rows),
        "slot0_forward",
        [VMEM] * len(first),
        [
            ((depth, 2 * width), BF16),
            ((depth, width), BF16),
            ((block, 2 * width), F32),
            ((block, width), BF16),
            ((block, depth), F32),
        ],
        *first,
    )
    (sent,) = call(
        functools.partial(gradient_kernel, groups, chips, cores, tokens, rows, span),
        "slot0_gradient",
        [VMEM] * (len(first) + len(second) + len(kept)),
        [((3, depth // cores, width), BF16)],
        *first,
        *second,
        *kept,
        scratch=[pltpu.VMEM((depth, 2 * width), BF16), pltpu.VMEM((depth, width), BF16)],
    )
    arrived = lax.ppermute(sent, "group", [(at, (at + 1) % groups) for at in range(groups)])
    zeros = call(
        functools.partial(query_kernel, chips, tokens),
        "slot0_queries",
        [VMEM] * (chips + 3),
        [((tokens, depth), BF16)] * chips,
        *asked,
        *kept[:2],
        norm_gain,
    )
    zeros = outward(zeros)
    outs = call(
        functools.partial(second_kernel, chips, cores, tokens, rows, span),
        "slot1",
        [VMEM] * (len(learn) + chips + cores + 1),
        [((tokens, depth), BF16)] * chips + [((3 * rows, width), BF16)] * chips,
        *learn,
        *asked,
        arrived,
        sibling(arrived),
        norm_gain,
        scratch=[
            pltpu.VMEM((depth, 2 * width), BF16),
            pltpu.VMEM((depth, width), BF16),
            pltpu.VMEM((depth, 2 * width), F32),
            pltpu.VMEM((depth, width), F32),
        ],
    )
    ones, states = outward(outs[:chips]), outward(outs[chips:])
    head_output, state_out = call(
        functools.partial(unpack_kernel, chips),
        "unpack",
        [VMEM] * (3 * chips),
        [((2, heads, tokens, depth), BF16), ((heads, 3, rows, width), F32)],
        *zeros,
        *ones,
        *states,
    )
    return head_output, jnp.transpose(state_out, (0, 2, 1, 3))[None]


def solution(mesh):
    groups, shards = mesh.shape["group"], mesh.shape["shard"]
    cores = 2 if shards % 2 == 0 else 1
    devices = np.asarray(mesh.devices).reshape(groups, shards // cores, cores)
    split = Mesh(devices, ("group", "chip", "core"))
    tokens = ("group", "chip", "core")
    shard = ("chip", "core")
    in_specs = (
        P(None, None, tokens, None),
        P(None, None, tokens, None),
        P(None, None, tokens, None),
        P(None, None, tokens),
        P("group", None, shard, None, None),
        P(None, shard, None, None),
        P(),
    )
    out_specs = (P(None, None, tokens, None), P("group", None, shard, None, None))
    return jax.shard_map(
        on_device, mesh=split, in_specs=in_specs, out_specs=out_specs, check_vma=False
    )
```
